32 devices in a mesh: segment: 4 (over y, x), blk: 8 (over z, core).
Axes of the slice: x: 2, y: 2, z: 4, core: 2. Of those that a mesh axis runs over, the one named last changes fastest.
Arguments:
- inputs: bfloat16 [4, 128, 64, 128], P(None, 'blk'), may hold values from -6 to 6
- weights: bfloat16 [8, 128, 64, 2048], P('segment', 'blk'), may hold values from -0.1875 to 0.1875
- biases: float32 [8, 128, 64], P('segment', 'blk'), may hold values from -3 to 3
- tile_index: int32 [8, 128, 32], P('segment', 'blk'), may hold values from 0 to 31, each once within a row
Outputs:
- final_activity: bfloat16 [4, 128, 64, 128], P('segment', 'blk')
The draws below stay inside these ranges and needn't reach their ends.
Inputs may be any that keep to these rules, and one draw needn't show every extreme that they name: `tile_index`: each row of 32 entries names every member 0..31 once.
All inputs are finite; a program needn't handle non-finite values.
Results may differ from the reference program's by a relative error of at most 0.014.
Values may be sent and summed in bfloat16 or wider, within the bound.
No kernel may reach another device: no remote copies, remote signals or barrier semaphores. Data moves between devices by JAX's collectives and lax.ppermute only.
A program may use at most 128 MiB of HBM per device.

```python
import jax
import jax.numpy as jnp
from jax import lax

TILE = 64
FANIN = 32
BATCH = 128
BLK_DEV = 16
BLOCKS = 128
GRP = 2
OUTER = 1
LAYERS = 8
MB = 4


def steps_of(key, extent, pieces, smallest, largest):
    def one(position, shards_of):
        draws = jax.random.uniform(jax.random.fold_in(jax.random.fold_in(key, 6), position), (shards_of,), jnp.float32, smallest / len(pieces), largest / len(pieces))
        return jnp.repeat(jnp.exp(draws), extent[position] // shards_of).reshape((-1,) + (1,) * (len(extent) - position - 1))

    level = one(*pieces[0])
    for cut in pieces[1:]:
        level = level * one(*cut)
    return level


def gaussian(stream_key, shape, width, reach, pieces=(), kind=jnp.bfloat16):
    drawn = width * jax.random.normal(stream_key, shape, jnp.float32)
    if pieces:
        drawn = drawn * steps_of(stream_key, shape, pieces, -0.22, 0.18)
    return jnp.clip(drawn, -reach, reach).astype(kind)


def setup_inputs(seed: int = 0) -> dict:
    streams_of = jax.random.split(jax.random.key(seed), 5)
    inputs = gaussian(streams_of[0], (MB, BLOCKS, TILE, BATCH), 1.0, 6.0, ((1, 8),))
    weights = gaussian(streams_of[1], (LAYERS, BLOCKS, TILE, FANIN * TILE), (FANIN * TILE // 2) ** -0.5, 0.1875, ((0, 4), (1, 8)))
    biases = gaussian(streams_of[2], (LAYERS, BLOCKS, TILE), 0.5, 3.0, ((0, 4), (1, 8)), jnp.float32)
    tile_index = jax.vmap(lambda own: jax.random.permutation(own, FANIN))(jax.random.split(streams_of[3], LAYERS * BLOCKS)).reshape((LAYERS, BLOCKS, FANIN)).astype(jnp.int32)
    return {"inputs": inputs, "weights": weights, "biases": biases, "tile_index": tile_index}


def group_layer(values, weight_groups, bias_groups, index_groups):
    def one_group(packed):
        group_values, group_weights, group_biases, group_index = packed
        onehot = (group_index[:, :, None] == jnp.arange(FANIN, dtype=jnp.int32)[None, None, :]).astype(jnp.float32)
        shaped = group_weights.astype(jnp.float32).reshape(FANIN, TILE, FANIN, TILE)
        placed = jnp.einsum("jakc,jkm->jamc", shaped, onehot, precision=lax.Precision.HIGHEST)
        placed = placed.reshape(FANIN * TILE, FANIN * TILE)
        flat_group = group_values.astype(jnp.float32).reshape(FANIN * TILE, -1)
        summed = jnp.dot(placed, flat_group, precision=lax.Precision.HIGHEST).reshape(FANIN, TILE, -1)
        summed = summed + group_biases[:, :, None]
        return jnp.maximum(summed, 0.0).astype(jnp.bfloat16)

    return lax.map(one_group, (values, weight_groups, bias_groups, index_groups))


def swap_digits(values):
    rest = values.shape[1:]
    shaped = values.reshape((OUTER * 2, GRP, 2, BLK_DEV // GRP, GRP) + rest)
    order = (0, 4, 2, 3, 1) + tuple(range(5, 5 + len(rest)))
    return shaped.transpose(order).reshape(values.shape)


def odd_groups(values):
    rest = values.shape[1:]
    shaped = values.reshape((OUTER, 2, GRP, 2, BLK_DEV) + rest)
    order = (0, 2, 3, 1, 4) + tuple(range(5, 5 + len(rest)))
    return shaped.transpose(order).reshape((BLOCKS // FANIN, FANIN) + rest)


def odd_ungroup(grouped):
    rest = grouped.shape[2:]
    shaped = grouped.reshape((OUTER, GRP, 2, 2, BLK_DEV) + rest)
    order = (0, 3, 1, 2, 4) + tuple(range(5, 5 + len(rest)))
    return shaped.transpose(order).reshape((BLOCKS,) + rest)


def even_groups(values):
    return values.reshape((BLOCKS // FANIN, FANIN) + values.shape[1:])


def reference(inputs, weights, biases, tile_index):
    values = jnp.transpose(inputs, (1, 2, 0, 3)).reshape(BLOCKS, TILE, MB * BATCH)
    for layer_index in range(LAYERS):
        if layer_index % 2 == 0:
            grouped = group_layer(even_groups(values), even_groups(weights[layer_index]),
                                  even_groups(biases[layer_index]), even_groups(tile_index[layer_index]))
            values = grouped.reshape(BLOCKS, TILE, MB * BATCH)
        else:
            swapped = swap_digits(values)
            grouped = group_layer(odd_groups(swapped), odd_groups(weights[layer_index]),
                                  odd_groups(biases[layer_index]), odd_groups(tile_index[layer_index]))
            values = swap_digits(odd_ungroup(grouped))
    return values.reshape(BLOCKS, TILE, MB, BATCH).transpose(2, 0, 1, 3)
```

```python
import functools

import jax
import jax.numpy as jnp
from jax import lax
from jax.experimental import pallas as pl
from jax.experimental.pallas import tpu as pltpu
from jax.sharding import PartitionSpec as P

VMEM_LIMIT = 40 * 1024 * 1024
WEIGHT_COPIES = 4


def place_kernel(layer, tile_ref, column_ref, row_ref, weights_ref, placed_ref, held, inverse, arrived):
    slots, _, tile, width = held.shape
    fan = tile_ref.shape[2]
    lanes = 2 * tile
    copies = arrived.shape[0]
    per_copy = slots // copies

    def copy(part):
        first = part * per_copy
        return pltpu.make_async_copy(
            weights_ref.at[layer, pl.ds(first, per_copy)], held.at[pl.ds(first, per_copy), 0], arrived.at[part]
        )

    for part in range(copies):
        copy(part).start()

    def invert(slot, carry):
        for k in range(fan):
            inverse[slot, column_ref[tile_ref[layer, slot, k]]] = k
        return carry

    lax.fori_loop(0, slots, invert, 0)
    low_half = lax.broadcasted_iota(jnp.int32, (tile, lanes), 1) < tile

    def place(slot, carry):
        for pair in range(width // lanes):
            columns = pl.ds(pair * lanes, lanes)
            both = held[slot, 0, :, columns]
            held[slot, 1, :, columns] = jnp.concatenate([both[:, tile:], both[:, :tile]], axis=1)
        row = pl.multiple_of(row_ref[slot] * tile, tile)
        for pair in range(width // lanes):
            low, high = inverse[slot, 2 * pair], inverse[slot, 2 * pair + 1]
            low_tile = held[slot, low & 1, :, pl.ds(pl.multiple_of((low >> 1) * lanes, lanes), lanes)]
            high_tile = held[slot, 1 - (high & 1), :, pl.ds(pl.multiple_of((high >> 1) * lanes, lanes), lanes)]
            placed_ref[pl.ds(row, tile), pl.ds(pair * lanes, lanes)] = jnp.where(low_half, low_tile, high_tile)
        return carry

    for part in range(copies):
        copy(part).wait()
        lax.fori_loop(part * per_copy, (part + 1) * per_copy, place, 0)


def placed_weights(layer, weights, tile_index, columns, rows):
    _, slots, tile, width = weights.shape
    copies = min(WEIGHT_COPIES, slots)
    return pl.pallas_call(
        functools.partial(place_kernel, layer),
        grid_spec=pltpu.PrefetchScalarGridSpec(
            num_scalar_prefetch=3,
            grid=(1,),
            in_specs=[pl.BlockSpec(memory_space=pl.ANY)],
            out_specs=pl.BlockSpec((slots * tile, width), lambda i, *_: (0, 0)),
            scratch_shapes=[
                pltpu.VMEM((slots, 2, tile, width), weights.dtype),
                pltpu.SMEM((slots, tile_index.shape[2]), jnp.int32),
                pltpu.SemaphoreType.DMA((copies,)),
            ],
        ),
        out_shape=jax.ShapeDtypeStruct((slots * tile, width), weights.dtype),
        compiler_params=pltpu.CompilerParams(vmem_limit_bytes=VMEM_LIMIT),
        name="place_tiles",
    )(tile_index, columns, rows, weights)


def layer_kernel(pieces, *refs):
    piece_refs, (matrix_ref, offset_ref), out_refs = refs[:pieces], refs[pieces : pieces + 2], refs[pieces + 2 :]
    rows = out_refs[0].shape[0]
    for part, out_ref in enumerate(out_refs):
        block = pl.ds(part * rows, rows)
        total = offset_ref[block, :]
        first = 0
        for piece_ref in piece_refs:
            depth = piece_ref.shape[0]
            total = total + jnp.dot(
                matrix_ref[block, pl.ds(first, depth)], piece_ref[...], preferred_element_type=jnp.float32
            )
            first += depth
        out_ref[...] = jnp.maximum(total, 0.0).astype(out_ref.dtype)


def layer(pieces, matrix, offset, parts):
    rows, width = matrix.shape
    batch = pieces[0].shape[1]
    whole = pl.BlockSpec(memory_space=pltpu.VMEM)
    return pl.pallas_call(
        functools.partial(layer_kernel, len(pieces)),
        in_specs=[whole] * (len(pieces) + 2),
        out_specs=[whole] * parts,
        out_shape=[jax.ShapeDtypeStruct((rows // parts, batch), pieces[0].dtype)] * parts,
        cost_estimate=pl.CostEstimate(
            flops=2 * rows * width * batch, bytes_accessed=2 * rows * width, transcendentals=0
        ),
        compiler_params=pltpu.CompilerParams(vmem_limit_bytes=VMEM_LIMIT),
        name="layer",
    )(*pieces, matrix, offset)


def body(inputs, weights, biases, tile_index):
    micro_count, local, tile, batch = inputs.shape
    fan = tile_index.shape[2]
    segments, devices = lax.axis_size("segment"), lax.axis_size("blk")
    group = min(local, devices // 4)
    deep = local // group
    part_rows = deep * tile
    segment, position = lax.axis_index("segment"), lax.axis_index("blk")
    core, near, far = position % 2, position // 2 % group, position // (2 * group) % 2

    member = jnp.arange(fan, dtype=jnp.int32)
    member_digit, member_slot = member // local, member % local
    slot_part, slot_deep = (member_slot % group) ^ near, member_slot // group
    in_part = slot_part * deep + slot_deep
    even_columns = (member_digit ^ core) * local + jnp.where(segment == 0, member_slot, in_part)
    odd_columns = (member_digit ^ far) * local + in_part
    rows = in_part[:local]
    matrices = [
        placed_weights(index, weights, tile_index, columns, rows)
        for index, columns in enumerate((even_columns, odd_columns))
    ]
    shaped = biases.reshape(biases.shape[0], deep, group, tile)
    shaped = jnp.take(shaped, jnp.arange(group) ^ near, axis=2).swapaxes(1, 2)
    offsets = jnp.broadcast_to(shaped.reshape(biases.shape[0], local * tile, 1), (biases.shape[0], local * tile, batch))

    def along(value, flip):
        return lax.ppermute(value, "blk", [(i, i ^ flip) for i in range(devices)])

    def exchange(parts):
        pieces = []
        for x in range(2 * group):
            part = parts[x % group]
            pieces.append(along(part, 2 * x) if x else part)
        return pieces

    def passed(parts, hops):
        return [
            lax.ppermute(
                part,
                ("segment", "blk"),
                [(s * devices + i, t * devices + (i ^ 2 * x)) for s, t in hops for i in range(devices)],
            )
            for x, part in enumerate(parts)
        ]

    steps = micro_count + segments - 1
    arriving = [jnp.zeros((part_rows, batch), inputs.dtype)] * group
    finished = []
    for step in range(steps):
        if step < micro_count:
            fresh = inputs[step].reshape(group, part_rows, batch)
            arriving = [jnp.where(segment == 0, fresh[x], arriving[x]) for x in range(group)]
        joined = arriving + [along(part, 1) for part in arriving]
        parts = layer(joined, matrices[0], offsets[0], group)
        parts = layer(exchange(parts), matrices[1], offsets[1], group)
        hops = [(s, s + 1) for s in range(segments - 1) if 0 <= step - s < micro_count]
        done = step - (segments - 1)
        if done >= 0:
            hops.append((segments - 1, done))
        arriving = passed(parts, hops)
        if done >= 0:
            finished.append(arriving)
    result = finished[0]
    for index in range(1, micro_count):
        result = [jnp.where(segment == index, new, old) for new, old in zip(finished[index], result)]
    stacked = jnp.stack(result).reshape(group, deep, tile, batch)
    stacked = jnp.take(stacked, jnp.arange(group) ^ near, axis=0)
    return stacked.swapaxes(0, 1).reshape(1, local, tile, batch)


def solution(mesh):
    in_specs = (
        P(None, "blk", None, None),
        P("segment", "blk", None, None),
        P("segment", "blk", None),
        P("segment", "blk", None),
    )
    out_specs = P("segment", "blk", None, None)
    return jax.shard_map(body, mesh=mesh, in_specs=in_specs, out_specs=out_specs, check_vma=False)
```

```python
import functools

import jax
import jax.numpy as jnp
from jax import lax
from jax.experimental import pallas as pl
from jax.experimental.pallas import tpu as pltpu
from jax.sharding import PartitionSpec as P

MIB = 1024 * 1024
PLACE_VMEM = 46 * MIB
LAYER_VMEM = 16 * MIB
WEIGHT_COPIES = 4
WHOLE = pl.BlockSpec(memory_space=pltpu.VMEM)
TABLE = pl.BlockSpec(memory_space=pltpu.SMEM)


def place_kernel(layer, order, tile_ref, column_ref, slot_ref, weights_ref, placed_ref, held, arrived):
    slots, tile, width = held.shape
    lanes = 2 * tile
    copies = arrived.shape[0]
    per_copy = slots // copies
    pairs = slots // 2 // copies

    def copy(part):
        these = pl.ds(part * per_copy, per_copy)
        return pltpu.make_async_copy(weights_ref.at[layer, these], held.at[these], arrived.at[part])

    def place(pair):
        both_slots = [slot_ref[2 * pair], slot_ref[2 * pair + 1]]
        for block in range(width // lanes):
            columns = pl.ds(block * lanes, lanes)
            turned = jnp.concatenate([held[slot, :, columns] for slot in both_slots], axis=0).T
            for half in range(2):
                for side, slot in enumerate(both_slots):
                    row = pl.multiple_of(column_ref[layer, tile_ref[layer, slot, 2 * block + half]] * tile, tile)
                    placed_ref[pair, pl.ds(row, tile), pl.ds(side * tile, tile)] = turned[
                        half * tile : (half + 1) * tile, side * tile : (side + 1) * tile
                    ]

    for part in range(copies):
        copy(part).start()
    for part in range(copies):
        copy(part).wait()
        for pair in order[part * pairs : (part + 1) * pairs]:
            place(pair)


def placed_weights(layer, weights, tile_index, columns, slots_of, order):
    _, slots, tile, width = weights.shape
    copies = min(WEIGHT_COPIES, slots // 2)
    return pl.pallas_call(
        functools.partial(place_kernel, layer, order),
        in_specs=[TABLE, TABLE, TABLE, pl.BlockSpec(memory_space=pltpu.HBM)],
        out_specs=WHOLE,
        out_shape=jax.ShapeDtypeStruct((slots // 2, width, 2 * tile), weights.dtype),
        scratch_shapes=[pltpu.VMEM((slots, tile, width), weights.dtype), pltpu.SemaphoreType.DMA((copies,))],
        compiler_params=pltpu.CompilerParams(vmem_limit_bytes=PLACE_VMEM),
        name="place_tiles",
    )(tile_index, columns, slots_of, weights)


def turn_kernel(blocks_ref, turned_ref):
    for index in range(blocks_ref.shape[0]):
        turned_ref[index] = blocks_ref[index].T


def turned(blocks):
    count, rows, columns = blocks.shape
    return pl.pallas_call(
        turn_kernel,
        in_specs=[WHOLE],
        out_specs=WHOLE,
        out_shape=jax.ShapeDtypeStruct((count, columns, rows), blocks.dtype),
        compiler_params=pltpu.CompilerParams(vmem_limit_bytes=LAYER_VMEM),
        name="turn",
    )(blocks)


def layer_kernel(pieces, parts, forwarders, *refs):
    piece_refs, (matrix_ref, offset_ref), refs = refs[:pieces], refs[pieces : pieces + 2], refs[pieces + 2 :]
    kept_refs, out_refs = refs[:-parts], refs[-parts:]
    pairs, _, lanes = matrix_ref.shape
    per_out = pairs // parts
    step = 2 if per_out % 2 == 0 else 1

    def compute():
        values = jnp.concatenate([piece[...] for piece in piece_refs], axis=1)
        for first in range(0, pairs, step):
            matrix = jnp.concatenate([matrix_ref[first + index] for index in range(step)], axis=1)
            total = jnp.dot(values, matrix, preferred_element_type=jnp.float32)
            total = total + offset_ref[:, pl.ds(first * lanes, step * lanes)]
            out_ref = out_refs[first // per_out]
            out_ref[:, pl.ds(first % per_out * lanes, step * lanes)] = jnp.maximum(total, 0.0).astype(out_ref.dtype)

    if not kept_refs:
        compute()
        return
    place_ref, *kept_refs = kept_refs

    @pl.when(place_ref[0] >= forwarders)
    def _():
        compute()

    @pl.when(place_ref[0] < forwarders)
    def _():
        for kept_ref, out_ref in zip(kept_refs, out_refs):
            out_ref[...] = kept_ref[...]


def layer(pieces, matrix, offset, parts, place, forwarders=0, kept=()):
    pairs, width, lanes = matrix.shape
    batch = pieces[0].shape[0]
    outs = parts if pairs % parts == 0 else 1
    extra, kept = ([place], list(kept)) if forwarders else ([], [])
    if outs < parts:
        pieces = [jnp.concatenate(pieces, axis=1)]
        kept = [jnp.concatenate(kept, axis=1)] if kept else []
    result = pl.pallas_call(
        functools.partial(layer_kernel, len(pieces), outs, forwarders),
        in_specs=[WHOLE] * (len(pieces) + 2) + [TABLE] * len(extra) + [WHOLE] * len(kept),
        out_specs=[WHOLE] * outs,
        out_shape=[jax.ShapeDtypeStruct((batch, pairs * lanes // outs), pieces[0].dtype)] * outs,
        cost_estimate=pl.CostEstimate(
            flops=2 * batch * width * pairs * lanes, bytes_accessed=2 * pairs * width * lanes, transcendentals=0
        ),
        compiler_params=pltpu.CompilerParams(vmem_limit_bytes=LAYER_VMEM),
        name="layer",
    )(*pieces, matrix, offset, *extra, *kept)
    return list(result) if outs == parts else jnp.split(result[0], parts, axis=1)


def finish_kernel(place_ref, *refs):
    out_ref = refs[-1]
    deep, group, tile, batch = out_ref.shape
    part_refs, exchanged_refs = refs[:group], refs[group:-1]
    odd = place_ref[0] % 2 == 1
    for x in range(group):
        value = part_refs[x][...]
        if x:
            value = jnp.where(odd, exchanged_refs[x - 1][...], value)
        out_ref[:, place_ref[1] ^ x] = value.T.reshape(deep, tile, batch)


def finished(parts, exchanged, place, shape):
    return pl.pallas_call(
        finish_kernel,
        in_specs=[TABLE] + [WHOLE] * (len(parts) + len(exchanged)),
        out_specs=WHOLE,
        out_shape=jax.ShapeDtypeStruct(shape, parts[0].dtype),
        compiler_params=pltpu.CompilerParams(vmem_limit_bytes=LAYER_VMEM),
        name="finish",
    )(place, *parts, *exchanged)


def body(inputs, weights, biases, tile_index):
    micro_count, local, tile, batch = inputs.shape
    fan = tile_index.shape[2]
    segments, devices = lax.axis_size("segment"), lax.axis_size("blk")
    assert micro_count == segments and segments % 2 == 0
    group = min(local, devices // 4)
    deep = local // group
    part_width = deep * tile
    segment, position = lax.axis_index("segment"), lax.axis_index("blk")
    core, near, far = position & 1, (position >> 1) & (group - 1), position // (2 * group) & 1

    member = jnp.arange(fan, dtype=jnp.int32)
    member_digit, member_slot = member // local, member % local
    in_part = ((member_slot % group) ^ near) * deep + member_slot // group
    even_columns = (member_digit ^ core) * local + jnp.where(segment == 0, member_slot, in_part)
    odd_columns = (member_digit ^ far) * local + in_part
    columns = jnp.stack([even_columns, odd_columns])
    spot = jnp.arange(local, dtype=jnp.int32)
    slots_of = spot % deep * group + ((spot // deep) ^ near)
    first_of = [(2 * pair) % deep * group if deep > 1 else 2 * pair for pair in range(local // 2)]
    order = sorted(range(local // 2), key=lambda pair: (first_of[pair], pair))
    offsets = biases.reshape(biases.shape[0], deep, group, tile)
    offsets = jnp.stack([lax.dynamic_index_in_dim(offsets, near ^ x, 2, keepdims=False) for x in range(group)], axis=1)
    offsets = offsets.reshape(biases.shape[0], 1, local * tile)
    place = jnp.stack([segment, near]).astype(jnp.int32)
    columns, slots_of, place, first, offsets = lax.optimization_barrier((columns, slots_of, place, segment == 0, offsets))
    matrices = [placed_weights(index, weights, tile_index, columns, slots_of, order) for index in range(2)]

    def along(value, flip):
        return lax.ppermute(value, "blk", [(i, i ^ flip) for i in range(devices)])

    def exchange(parts):
        pieces = {0: parts[0]}
        for x in [*range(group, 2 * group), *range(1, group)]:
            pieces[x] = along(parts[x % group], 2 * x)
        return [pieces[x] for x in range(2 * group)]

    def passed(parts):
        return [
            lax.ppermute(
                part,
                ("segment", "blk"),
                [(s * devices + i, (s + 1) % segments * devices + (i ^ 2 * x)) for s in range(segments) for i in range(devices)],
            )
            for x, part in enumerate(parts)
        ]

    sequence = [*range(segments - 2, -1, -1), segments - 1]
    turns = micro_count + segments - 1
    arriving = ()
    for turn in range(turns):
        if turn == 0:
            new = inputs[sequence[turn]].reshape(local * tile, batch)
            pieces = list(turned(jnp.stack([new, along(new, 1)])))
        elif turn < micro_count:
            new = turned(inputs[sequence[turn]].reshape(1, local * tile, batch))[0]
            new = [new[:, x * part_width : (x + 1) * part_width] for x in range(group)]
            pieces = [jnp.where(first, a, b) for a, b in zip(new, arriving)]
        else:
            pieces = arriving
        if turn:
            pieces = pieces + [along(part, 1) for part in pieces]
        parts = layer(pieces, matrices[0], offsets[0], group, place)
        pieces = exchange(parts)
        forwarders = max(0, turn - micro_count + 1)
        parts = layer(pieces, matrices[1], offsets[1], group, place, forwarders, arriving)
        if turn < turns - 1:
            arriving = passed(parts)

    exchanged = [along(parts[x], 2 * x) for x in range(1, group)]
    return finished(parts, exchanged, place, (deep, group, tile, batch)).reshape(1, local, tile, batch)


def solution(mesh):
    in_specs = (
        P(None, "blk", None, None),
        P("segment", "blk", None, None),
        P("segment", "blk", None),
        P("segment", "blk", None),
    )
    out_specs = P("segment", "blk", None, None)
    return jax.shard_map(body, mesh=mesh, in_specs=in_specs, out_specs=out_specs, check_vma=False)
```

```python
import functools

import jax
import jax.numpy as jnp
from jax import lax
from jax.experimental import pallas as pl
from jax.experimental.pallas import tpu as pltpu
from jax.sharding import PartitionSpec as P

MIB = 1024 * 1024
PLACE_VMEM = 46 * MIB
LAYER_VMEM = 16 * MIB
WEIGHT_COPIES = 4
WHOLE = pl.BlockSpec(memory_space=pltpu.VMEM)
TABLE = pl.BlockSpec(memory_space=pltpu.SMEM)


def place_kernel(layer, order, column_ref, slot_ref, bias_ref, index_ref, weights_ref, placed_ref, row_ref, held, tile_ref, arrived, listed):
    slots, tile, width = held.shape
    lanes = 2 * tile
    copies = arrived.shape[0]
    per_copy = slots // copies
    pairs = slots // 2 // copies

    def copy(part):
        these = pl.ds(part * per_copy, per_copy)
        return pltpu.make_async_copy(weights_ref.at[layer, these], held.at[these], arrived.at[part])

    def place(pair):
        both_slots = [slot_ref[2 * pair], slot_ref[2 * pair + 1]]
        for block in range(width // lanes):
            columns = pl.ds(block * lanes, lanes)
            turned = jnp.concatenate([held[slot, :, columns] for slot in both_slots], axis=0).T
            for half in range(2):
                for side, slot in enumerate(both_slots):
                    row = pl.multiple_of(column_ref[layer, tile_ref[slot, 2 * block + half]] * tile, tile)
                    placed_ref[pair, pl.ds(row, tile), pl.ds(side * tile, tile)] = turned[
                        half * tile : (half + 1) * tile, side * tile : (side + 1) * tile
                    ]

    listing = pltpu.make_async_copy(index_ref.at[layer], tile_ref, listed)
    listing.start()
    for part in range(copies):
        copy(part).start()
    for spot in range(slots):
        row_ref[:, pl.ds(spot * tile, tile)] = bias_ref[layer, pl.ds(slot_ref[spot], 1), :]
    listing.wait()
    for part in range(copies):
        copy(part).wait()
        for pair in order[part * pairs : (part + 1) * pairs]:
            place(pair)


def placed(layer, weights, biases, tile_index, columns, slots_of, order):
    _, slots, tile, width = weights.shape
    copies = min(WEIGHT_COPIES, slots // 2)
    away = pl.BlockSpec(memory_space=pltpu.HBM)
    return pl.pallas_call(
        functools.partial(place_kernel, layer, order),
        in_specs=[TABLE, TABLE, WHOLE, away, away],
        out_specs=[WHOLE, WHOLE],
        out_shape=[
            jax.ShapeDtypeStruct((slots // 2, width, 2 * tile), weights.dtype),
            jax.ShapeDtypeStruct((1, slots * tile), biases.dtype),
        ],
        scratch_shapes=[
            pltpu.VMEM((slots, tile, width), weights.dtype),
            pltpu.SMEM(tile_index.shape[1:], tile_index.dtype),
            pltpu.SemaphoreType.DMA((copies,)),
            pltpu.SemaphoreType.DMA(()),
        ],
        compiler_params=pltpu.CompilerParams(vmem_limit_bytes=PLACE_VMEM),
        name="place_tiles",
    )(columns, slots_of, biases, tile_index, weights)


def turn_kernel(micro, *refs):
    for blocks_ref, turned_ref in zip(refs[: len(refs) // 2], refs[len(refs) // 2 :]):
        turned_ref[...] = blocks_ref[micro].T


def turned(arrays, micro):
    _, rows, columns = arrays[0].shape
    return pl.pallas_call(
        functools.partial(turn_kernel, micro),
        in_specs=[WHOLE] * len(arrays),
        out_specs=[WHOLE] * len(arrays),
        out_shape=[jax.ShapeDtypeStruct((columns, rows), arrays[0].dtype)] * len(arrays),
        compiler_params=pltpu.CompilerParams(vmem_limit_bytes=LAYER_VMEM),
        name="turn",
    )(*arrays)


def product(piece_refs, matrix_ref, first, step, depth):
    values = jnp.concatenate([piece[...] for piece in piece_refs], axis=1)
    rows = pl.ds(depth, values.shape[1])
    matrix = jnp.concatenate([matrix_ref[first + index, rows, :] for index in range(step)], axis=1)
    return jnp.dot(values, matrix, preferred_element_type=jnp.float32)


def early_kernel(*refs):
    *piece_refs, matrix_ref, offset_ref, total_ref = refs
    pairs, _, lanes = matrix_ref.shape
    step = 2 if pairs % 2 == 0 else 1
    for first in range(0, pairs, step):
        columns = pl.ds(first * lanes, step * lanes)
        total_ref[:, columns] = product(piece_refs, matrix_ref, first, step, 0) + offset_ref[:, columns]


def layer_kernel(pieces, parts, depth, forwarders, *refs):
    piece_refs, (matrix_ref, start_ref), refs = refs[:pieces], refs[pieces : pieces + 2], refs[pieces + 2 :]
    kept_refs, out_refs = refs[:-parts], refs[-parts:]
    pairs, _, lanes = matrix_ref.shape
    per_out = pairs // parts
    step = 2 if per_out % 2 == 0 else 1
    for first in range(0, pairs, step):
        total = product(piece_refs, matrix_ref, first, step, depth) + start_ref[:, pl.ds(first * lanes, step * lanes)]
        total = jnp.maximum(total, 0.0)
        part, columns = first // per_out, pl.ds(first % per_out * lanes, step * lanes)
        if kept_refs:
            place_ref, *held_refs = kept_refs
            hands_on = place_ref[0, :1, : step * lanes] < forwarders
            total = jnp.where(hands_on, held_refs[part][:, columns].astype(jnp.float32), total)
        out_refs[part][:, columns] = total.astype(out_refs[part].dtype)


def layer(pieces, matrix, offset, parts, late=0, place=None, forwarders=0, kept=()):
    pairs, width, lanes = matrix.shape
    batch, kind = pieces[0].shape[0], pieces[0].dtype
    outs = parts if pairs % parts == 0 else 1
    extra, kept = ([place], list(kept)) if forwarders else ([], [])
    early, pieces = (pieces[:-late], pieces[-late:]) if late else ([], pieces)
    if outs < parts:
        early, pieces, kept = [[jnp.concatenate(some, axis=1)] if some else [] for some in (early, pieces, kept)]
    params = pltpu.CompilerParams(vmem_limit_bytes=LAYER_VMEM)

    def cost(depth):
        flops, moved = 2 * batch * depth * pairs * lanes, 2 * pairs * depth * lanes
        return pl.CostEstimate(flops=flops, bytes_accessed=moved, transcendentals=0)

    depth = sum(piece.shape[1] for piece in early)
    start = offset
    if early:
        start = pl.pallas_call(
            early_kernel,
            in_specs=[WHOLE] * (len(early) + 2),
            out_specs=WHOLE,
            out_shape=jax.ShapeDtypeStruct((batch, pairs * lanes), jnp.float32),
            cost_estimate=cost(depth),
            compiler_params=params,
            name="layer_early",
        )(*early, matrix, offset)
    result = pl.pallas_call(
        functools.partial(layer_kernel, len(pieces), outs, depth, forwarders),
        in_specs=[WHOLE] * (len(pieces) + 2 + len(extra) + len(kept)),
        out_specs=[WHOLE] * outs,
        out_shape=[jax.ShapeDtypeStruct((batch, pairs * lanes // outs), kind)] * outs,
        cost_estimate=cost(width - depth),
        compiler_params=params,
        name="layer",
    )(*pieces, matrix, start, *extra, *kept)
    return list(result) if outs == parts else jnp.split(result[0], parts, axis=1)


def finish_kernel(place_ref, *refs):
    out_ref = refs[-1]
    deep, group, tile, batch = out_ref.shape
    part_refs, exchanged_refs = refs[:group], refs[group:-1]
    odd = place_ref[0, :1, :batch] % 2 == 1
    near = place_ref[1, :1, :batch]
    values = [part.T for part in [ref[...] for ref in part_refs]]
    for x in range(1, group):
        values[x] = jnp.where(odd, exchanged_refs[x - 1][...].T, values[x])
    for e in range(group):
        value = values[e]
        for digit in range(1, group):
            value = jnp.where(near == digit, values[e ^ digit], value)
        out_ref[:, e] = value.reshape(deep, tile, batch)


def finished(parts, exchanged, place, shape):
    return pl.pallas_call(
        finish_kernel,
        in_specs=[WHOLE] * (1 + len(parts) + len(exchanged)),
        out_specs=WHOLE,
        out_shape=jax.ShapeDtypeStruct(shape, parts[0].dtype),
        compiler_params=pltpu.CompilerParams(vmem_limit_bytes=LAYER_VMEM),
        name="finish",
    )(place, *parts, *exchanged)


def body(inputs, weights, biases, tile_index):
    micro_count, local, tile, batch = inputs.shape
    fan = tile_index.shape[2]
    segments, devices = lax.axis_size("segment"), lax.axis_size("blk")
    assert micro_count == segments and segments % 2 == 0
    group = min(local, devices // 4)
    deep = local // group
    part_width = deep * tile
    segment, position = lax.axis_index("segment"), lax.axis_index("blk")
    core, near, far = position & 1, (position >> 1) & (group - 1), position // (2 * group) & 1

    member = jnp.arange(fan, dtype=jnp.int32)
    member_digit, member_slot = member // local, member % local
    in_part = ((member_slot % group) ^ near) * deep + member_slot // group
    even_columns = (member_digit ^ core) * local + jnp.where(segment == 0, member_slot, in_part)
    part, across = (member_slot % group) ^ near, member_digit ^ far
    odd_piece = jnp.where(across == 0, jnp.where(part == 0, 0, 1 + part), jnp.where(part == 0, 1, group + part))
    odd_columns = odd_piece * deep + member_slot // group
    columns = jnp.stack([even_columns, odd_columns])
    spot = jnp.arange(local, dtype=jnp.int32)
    slots_of = spot % deep * group + ((spot // deep) ^ near)
    first_of = [(2 * pair) % deep * group if deep > 1 else 2 * pair for pair in range(local // 2)]
    order = sorted(range(local // 2), key=lambda pair: (first_of[pair], pair))
    place = jnp.broadcast_to(jnp.stack([segment, near]).astype(jnp.int32)[:, None, None], (2, 8, max(batch, 4 * tile)))
    columns, slots_of, place, first = lax.optimization_barrier((columns, slots_of, place, segment == 0))
    layers = [placed(index, weights, biases, tile_index, columns, slots_of, order) for index in range(2)]

    def along(value, flip):
        return lax.ppermute(value, "blk", [(i, i ^ flip) for i in range(devices)])

    def exchange(parts):
        pieces = {0: parts[0]}
        for x in range(1, 2 * group):
            pieces[x] = along(parts[x % group], 2 * x)
        return [pieces[x] for x in (0, group, *range(1, group), *range(group + 1, 2 * group))]

    def passed(parts):
        return [
            lax.ppermute(
                part,
                ("segment", "blk"),
                [(s * devices + i, (s + 1) % segments * devices + (i ^ 2 * x)) for s in range(segments) for i in range(devices)],
            )
            for x, part in enumerate(parts)
        ]

    sequence = [*range(segments - 2, -1, -1), segments - 1]
    turns = micro_count + segments - 1
    fresh = inputs.reshape(micro_count, local * tile, batch)
    arriving = ()
    for turn in range(turns):
        if turn == 0:
            pieces = turned([fresh, along(fresh, 1)], sequence[turn])
        elif turn < micro_count:
            (new,) = turned([fresh], sequence[turn])
            new = [new[:, x * part_width : (x + 1) * part_width] for x in range(group)]
            pieces = [jnp.where(first, a, b) for a, b in zip(new, arriving)]
        else:
            pieces = arriving
        if turn:
            pieces = pieces + [along(part, 1) for part in pieces]
        parts = layer(pieces, *layers[0], group, 1 if turn else 0)
        pieces = exchange(parts)
        forwarders = max(0, turn - micro_count + 1)
        parts = layer(pieces, *layers[1], group, 1, place, forwarders, arriving)
        if turn < turns - 1:
            arriving = passed(parts)

    exchanged = [along(parts[x], 2 * x) for x in range(1, group)]
    return finished(parts, exchanged, place, (deep, group, tile, batch)).reshape(1, local, tile, batch)


def solution(mesh):
    in_specs = (
        P(None, "blk", None, None),
        P("segment", "blk", None, None),
        P("segment", "blk", None),
        P("segment", "blk", None),
    )
    out_specs = P("segment", "blk", None, None)
    return jax.shard_map(body, mesh=mesh, in_specs=in_specs, out_specs=out_specs, check_vma=False)
```

```python
import functools

import jax
import jax.numpy as jnp
from jax import lax
from jax.experimental import pallas as pl
from jax.experimental.pallas import tpu as pltpu
from jax.sharding import PartitionSpec as P

MIB = 1024 * 1024
PLACE_VMEM = 46 * MIB
LAYER_VMEM = 16 * MIB
WHOLE = pl.BlockSpec(memory_space=pltpu.VMEM)
TABLE = pl.BlockSpec(memory_space=pltpu.SMEM)


def place_kernel(layer, order, column_ref, slot_ref, bias_ref, index_ref, weights_ref, placed_ref, row_ref, held, tile_ref, arrived, listed):
    slots, tile, width = held.shape
    lanes = 2 * tile
    copies = arrived.shape[0]
    per_copy = slots // copies
    pairs = slots // 2 // copies

    def copy(part):
        these = pl.ds(part * per_copy, per_copy)
        return pltpu.make_async_copy(weights_ref.at[layer, these], held.at[these], arrived.at[part])

    def place(pair):
        both_slots = [slot_ref[2 * pair], slot_ref[2 * pair + 1]]
        for block in range(width // lanes):
            columns = pl.ds(block * lanes, lanes)
            turned = jnp.concatenate([held[slot, :, columns] for slot in both_slots], axis=0).T
            for half in range(2):
                for side, slot in enumerate(both_slots):
                    row = pl.multiple_of(column_ref[layer, tile_ref[slot, 2 * block + half]] * tile, tile)
                    placed_ref[pair, pl.ds(row, tile), pl.ds(side * tile, tile)] = turned[
                        half * tile : (half + 1) * tile, side * tile : (side + 1) * tile
                    ]

    listing = pltpu.make_async_copy(index_ref.at[layer], tile_ref, listed)
    listing.start()
    for part in range(copies):
        copy(part).start()
    for spot in range(slots):
        row_ref[:, pl.ds(spot * tile, tile)] = bias_ref[layer, pl.ds(slot_ref[spot], 1), :]
    listing.wait()
    for part in range(copies):
        copy(part).wait()
        for pair in order[part * pairs : (part + 1) * pairs]:
            place(pair)


def placed(layer, weights, biases, tile_index, columns, slots_of, order, copies):
    _, slots, tile, width = weights.shape
    away = pl.BlockSpec(memory_space=pltpu.HBM)
    return pl.pallas_call(
        functools.partial(place_kernel, layer, order),
        in_specs=[TABLE, TABLE, WHOLE, away, away],
        out_specs=[WHOLE, WHOLE],
        out_shape=[
            jax.ShapeDtypeStruct((slots // 2, width, 2 * tile), weights.dtype),
            jax.ShapeDtypeStruct((1, slots * tile), biases.dtype),
        ],
        scratch_shapes=[
            pltpu.VMEM((slots, tile, width), weights.dtype),
            pltpu.SMEM(tile_index.shape[1:], tile_index.dtype),
            pltpu.SemaphoreType.DMA((copies,)),
            pltpu.SemaphoreType.DMA(()),
        ],
        compiler_params=pltpu.CompilerParams(vmem_limit_bytes=PLACE_VMEM),
        name="place_tiles",
    )(columns, slots_of, biases, tile_index, weights)


def turn_kernel(micro, *refs):
    for blocks_ref, turned_ref in zip(refs[: len(refs) // 2], refs[len(refs) // 2 :]):
        turned_ref[...] = blocks_ref[micro].T


def turned(arrays, micro):
    _, rows, columns = arrays[0].shape
    return pl.pallas_call(
        functools.partial(turn_kernel, micro),
        in_specs=[WHOLE] * len(arrays),
        out_specs=[WHOLE] * len(arrays),
        out_shape=[jax.ShapeDtypeStruct((columns, rows), arrays[0].dtype)] * len(arrays),
        compiler_params=pltpu.CompilerParams(vmem_limit_bytes=LAYER_VMEM),
        name="turn",
    )(*arrays)


def product(piece_refs, matrix_ref, first, step, depth):
    values = jnp.concatenate([piece[...] for piece in piece_refs], axis=1)
    rows = pl.ds(depth, values.shape[1])
    matrix = jnp.concatenate([matrix_ref[first + index, rows, :] for index in range(step)], axis=1)
    return jnp.dot(values, matrix, preferred_element_type=jnp.float32)


def early_kernel(*refs):
    *piece_refs, matrix_ref, offset_ref, total_ref = refs
    pairs, _, lanes = matrix_ref.shape
    step = 2 if pairs % 2 == 0 else 1
    for first in range(0, pairs, step):
        columns = pl.ds(first * lanes, step * lanes)
        total_ref[:, columns] = product(piece_refs, matrix_ref, first, step, 0) + offset_ref[:, columns]


def layer_kernel(pieces, parts, depth, forwarders, *refs):
    piece_refs, (matrix_ref, start_ref), refs = refs[:pieces], refs[pieces : pieces + 2], refs[pieces + 2 :]
    kept_refs, out_refs = refs[:-parts], refs[-parts:]
    pairs, _, lanes = matrix_ref.shape
    per_out = pairs // parts
    step = 2 if per_out % 2 == 0 else 1
    for first in range(0, pairs, step):
        total = product(piece_refs, matrix_ref, first, step, depth) + start_ref[:, pl.ds(first * lanes, step * lanes)]
        total = jnp.maximum(total, 0.0)
        part, columns = first // per_out, pl.ds(first % per_out * lanes, step * lanes)
        if kept_refs:
            place_ref, *held_refs = kept_refs
            hands_on = place_ref[0, :1, : step * lanes] < forwarders
            total = jnp.where(hands_on, held_refs[part][:, columns].astype(jnp.float32), total)
        out_refs[part][:, columns] = total.astype(out_refs[part].dtype)


def layer(pieces, matrix, offset, parts, late=0, place=None, forwarders=0, kept=()):
    pairs, width, lanes = matrix.shape
    batch, kind = pieces[0].shape[0], pieces[0].dtype
    outs = parts if pairs % parts == 0 else 1
    extra, kept = ([place], list(kept)) if forwarders else ([], [])
    early, pieces = (pieces[:-late], pieces[-late:]) if late else ([], pieces)
    if outs < parts:
        early, pieces, kept = [[jnp.concatenate(some, axis=1)] if some else [] for some in (early, pieces, kept)]
    params = pltpu.CompilerParams(vmem_limit_bytes=LAYER_VMEM)

    def cost(depth):
        flops, moved = 2 * batch * depth * pairs * lanes, 2 * pairs * depth * lanes
        return pl.CostEstimate(flops=flops, bytes_accessed=moved, transcendentals=0)

    depth = sum(piece.shape[1] for piece in early)
    start = offset
    if early:
        start = pl.pallas_call(
            early_kernel,
            in_specs=[WHOLE] * (len(early) + 2),
            out_specs=WHOLE,
            out_shape=jax.ShapeDtypeStruct((batch, pairs * lanes), jnp.float32),
            cost_estimate=cost(depth),
            compiler_params=params,
            name="layer_early",
        )(*early, matrix, offset)
    result = pl.pallas_call(
        functools.partial(layer_kernel, len(pieces), outs, depth, forwarders),
        in_specs=[WHOLE] * (len(pieces) + 2 + len(extra) + len(kept)),
        out_specs=[WHOLE] * outs,
        out_shape=[jax.ShapeDtypeStruct((batch, pairs * lanes // outs), kind)] * outs,
        cost_estimate=cost(width - depth),
        compiler_params=params,
        name="layer",
    )(*pieces, matrix, start, *extra, *kept)
    return list(result) if outs == parts else jnp.split(result[0], parts, axis=1)


def finish_kernel(place_ref, *refs):
    out_ref = refs[-1]
    deep, group, tile, batch = out_ref.shape
    part_refs, exchanged_refs = refs[:group], refs[group:-1]
    odd = place_ref[0, :1, :batch] % 2 == 1
    near = place_ref[1, :1, :batch]
    values = [part.T for part in [ref[...] for ref in part_refs]]
    for x in range(1, group):
        values[x] = jnp.where(odd, exchanged_refs[x - 1][...].T, values[x])
    for e in range(group):
        value = values[e]
        for digit in range(1, group):
            value = jnp.where(near == digit, values[e ^ digit], value)
        out_ref[:, e] = value.reshape(deep, tile, batch)


def finished(parts, exchanged, place, shape):
    return pl.pallas_call(
        finish_kernel,
        in_specs=[WHOLE] * (1 + len(parts) + len(exchanged)),
        out_specs=WHOLE,
        out_shape=jax.ShapeDtypeStruct(shape, parts[0].dtype),
        compiler_params=pltpu.CompilerParams(vmem_limit_bytes=LAYER_VMEM),
        name="finish",
    )(place, *parts, *exchanged)


def body(inputs, weights, biases, tile_index):
    micro_count, local, tile, batch = inputs.shape
    fan = tile_index.shape[2]
    segments, devices = lax.axis_size("segment"), lax.axis_size("blk")
    assert micro_count == segments and segments % 2 == 0
    group = min(local, devices // 4)
    deep = local // group
    part_width = deep * tile
    segment, position = lax.axis_index("segment"), lax.axis_index("blk")
    core, near, far = position & 1, (position >> 1) & (group - 1), position // (2 * group) & 1

    member = jnp.arange(fan, dtype=jnp.int32)
    member_digit, member_slot = member // local, member % local
    in_part = ((member_slot % group) ^ near) * deep + member_slot // group
    even_columns = (member_digit ^ core) * local + jnp.where(segment == 0, member_slot, in_part)
    part, across = (member_slot % group) ^ near, member_digit ^ far
    odd_piece = jnp.where(across == 0, jnp.where(part == 0, 0, 1 + part), jnp.where(part == 0, 1, group + part))
    odd_columns = odd_piece * deep + member_slot // group
    columns = jnp.stack([even_columns, odd_columns])
    spot = jnp.arange(local, dtype=jnp.int32)
    slots_of = spot % deep * group + ((spot // deep) ^ near)
    copies = max(1, deep // 2)
    order = sorted(range(local // 2), key=lambda pair: (2 * pair % deep, pair))
    place = jnp.broadcast_to(jnp.stack([segment, near]).astype(jnp.int32)[:, None, None], (2, 8, max(batch, 4 * tile)))
    columns, slots_of, place, first = lax.optimization_barrier((columns, slots_of, place, segment == 0))
    layers = [placed(index, weights, biases, tile_index, columns, slots_of, order, copies) for index in range(2)]

    def along(value, flip):
        return lax.ppermute(value, "blk", [(i, i ^ flip) for i in range(devices)])

    def exchange(parts):
        pieces = {0: parts[0]}
        for x in range(1, 2 * group):
            pieces[x] = along(parts[x % group], 2 * x)
        return [pieces[x] for x in (0, group, *range(1, group), *range(group + 1, 2 * group))]

    def passed(parts):
        return [
            lax.ppermute(
                part,
                ("segment", "blk"),
                [(s * devices + i, (s + 1) % segments * devices + (i ^ 2 * x)) for s in range(segments) for i in range(devices)],
            )
            for x, part in enumerate(parts)
        ]

    sequence = [*range(segments - 2, -1, -1), segments - 1]
    turns = micro_count + segments - 1
    fresh = inputs.reshape(micro_count, local * tile, batch)
    arriving = ()
    for turn in range(turns):
        if turn == 0:
            pieces = turned([fresh, along(fresh, 1)], sequence[turn])
        elif turn < micro_count:
            (new,) = turned([fresh], sequence[turn])
            new = [new[:, x * part_width : (x + 1) * part_width] for x in range(group)]
            pieces = [jnp.where(first, a, b) for a, b in zip(new, arriving)]
        else:
            pieces = arriving
        if turn:
            pieces = pieces + [along(part, 1) for part in pieces]
        parts = layer(pieces, *layers[0], group, 1 if turn else 0)
        pieces = exchange(parts)
        forwarders = max(0, turn - micro_count + 1)
        parts = layer(pieces, *layers[1], group, 1, place, forwarders, arriving)
        if turn < turns - 1:
            arriving = passed(parts)

    exchanged = [along(parts[x], 2 * x) for x in range(1, group)]
    return finished(parts, exchanged, place, (deep, group, tile, batch)).reshape(1, local, tile, batch)


def solution(mesh):
    in_specs = (
        P(None, "blk", None, None),
        P("segment", "blk", None, None),
        P("segment", "blk", None),
        P("segment", "blk", None),
    )
    out_specs = P("segment", "blk", None, None)
    return jax.shard_map(body, mesh=mesh, in_specs=in_specs, out_specs=out_specs, check_vma=False)
```

```python
import functools

import jax
import jax.numpy as jnp
from jax import lax
from jax.experimental import pallas as pl
from jax.experimental.pallas import tpu as pltpu
from jax.sharding import PartitionSpec as P

MIB = 1024 * 1024
PLACE_VMEM = 46 * MIB
LAYER_VMEM = 16 * MIB
WHOLE = pl.BlockSpec(memory_space=pltpu.VMEM)
TABLE = pl.BlockSpec(memory_space=pltpu.SMEM)


def place_kernel(layer, order, column_ref, slot_ref, index_ref, weights_ref, placed_ref, held, tile_ref, arrived, listed):
    slots, tile, width = held.shape
    lanes = 2 * tile
    copies = arrived.shape[0]
    per_copy = slots // copies
    pairs = slots // 2 // copies

    def copy(part):
        these = pl.ds(part * per_copy, per_copy)
        return pltpu.make_async_copy(weights_ref.at[layer, these], held.at[these], arrived.at[part])

    def place(pair):
        both_slots = [slot_ref[2 * pair], slot_ref[2 * pair + 1]]
        for block in range(width // lanes):
            columns = pl.ds(block * lanes, lanes)
            turned = jnp.concatenate([held[slot, :, columns] for slot in both_slots], axis=0).T
            for half in range(2):
                for side, slot in enumerate(both_slots):
                    row = pl.multiple_of(column_ref[layer, tile_ref[slot, 2 * block + half]] * tile, tile)
                    placed_ref[pair, pl.ds(row, tile), pl.ds(side * tile, tile)] = turned[
                        half * tile : (half + 1) * tile, side * tile : (side + 1) * tile
                    ]

    listing = pltpu.make_async_copy(index_ref.at[layer], tile_ref, listed)
    listing.start()
    for part in range(copies):
        copy(part).start()
    listing.wait()
    for part in range(copies):
        copy(part).wait()
        for pair in order[part * pairs : (part + 1) * pairs]:
            place(pair)


def placed(layer, weights, tile_index, columns, slots_of, order, copies):
    _, slots, tile, width = weights.shape
    away = pl.BlockSpec(memory_space=pltpu.HBM)
    return pl.pallas_call(
        functools.partial(place_kernel, layer, order),
        in_specs=[TABLE, TABLE, away, away],
        out_specs=WHOLE,
        out_shape=jax.ShapeDtypeStruct((slots // 2, width, 2 * tile), weights.dtype),
        scratch_shapes=[
            pltpu.VMEM((slots, tile, width), weights.dtype),
            pltpu.SMEM(tile_index.shape[1:], tile_index.dtype),
            pltpu.SemaphoreType.DMA((copies,)),
            pltpu.SemaphoreType.DMA(()),
        ],
        compiler_params=pltpu.CompilerParams(vmem_limit_bytes=PLACE_VMEM),
        name="place_tiles",
    )(columns, slots_of, tile_index, weights)


def rows_kernel(group, bias_ref, place_ref, *row_refs):
    _, slots, tile = bias_ref.shape
    deep = slots // group
    near = place_ref[1, :1, :tile]
    for layer, row_ref in enumerate(row_refs):
        for spot in range(slots):
            x, d = spot // deep, spot % deep
            value = bias_ref[layer, pl.ds(d * group + x, 1), :]
            for digit in range(1, group):
                value = jnp.where(near == digit, bias_ref[layer, pl.ds(d * group + (x ^ digit), 1), :], value)
            row_ref[:, pl.ds(spot * tile, tile)] = value


def rows_of(biases, place, group):
    layers, slots, tile = biases.shape
    return pl.pallas_call(
        functools.partial(rows_kernel, group),
        in_specs=[WHOLE] * 2,
        out_specs=[WHOLE] * layers,
        out_shape=[jax.ShapeDtypeStruct((1, slots * tile), biases.dtype)] * layers,
        compiler_params=pltpu.CompilerParams(vmem_limit_bytes=LAYER_VMEM),
        name="bias_rows",
    )(biases, place)


def turn_kernel(micro, *refs):
    for blocks_ref, turned_ref in zip(refs[: len(refs) // 2], refs[len(refs) // 2 :]):
        turned_ref[...] = blocks_ref[micro].T


def turned(arrays, micro):
    _, rows, columns = arrays[0].shape
    return pl.pallas_call(
        functools.partial(turn_kernel, micro),
        in_specs=[WHOLE] * len(arrays),
        out_specs=[WHOLE] * len(arrays),
        out_shape=[jax.ShapeDtypeStruct((columns, rows), arrays[0].dtype)] * len(arrays),
        compiler_params=pltpu.CompilerParams(vmem_limit_bytes=LAYER_VMEM),
        name="turn",
    )(*arrays)


def product(piece_refs, matrix_ref, first, step, depth):
    values = jnp.concatenate([piece[...] for piece in piece_refs], axis=1)
    rows = pl.ds(depth, values.shape[1])
    matrix = jnp.concatenate([matrix_ref[first + index, rows, :] for index in range(step)], axis=1)
    return jnp.dot(values, matrix, preferred_element_type=jnp.float32)


def early_kernel(*refs):
    *piece_refs, matrix_ref, offset_ref, total_ref = refs
    pairs, _, lanes = matrix_ref.shape
    step = 2 if pairs % 2 == 0 else 1
    for first in range(0, pairs, step):
        columns = pl.ds(first * lanes, step * lanes)
        total_ref[:, columns] = product(piece_refs, matrix_ref, first, step, 0) + offset_ref[:, columns]


def layer_kernel(pieces, parts, depth, forwarders, *refs):
    piece_refs, (matrix_ref, start_ref), refs = refs[:pieces], refs[pieces : pieces + 2], refs[pieces + 2 :]
    kept_refs, out_refs = refs[:-parts], refs[-parts:]
    pairs, _, lanes = matrix_ref.shape
    per_out = pairs // parts
    step = 2 if per_out % 2 == 0 else 1
    for first in range(0, pairs, step):
        total = product(piece_refs, matrix_ref, first, step, depth) + start_ref[:, pl.ds(first * lanes, step * lanes)]
        total = jnp.maximum(total, 0.0)
        part, columns = first // per_out, pl.ds(first % per_out * lanes, step * lanes)
        if kept_refs:
            place_ref, *held_refs = kept_refs
            hands_on = place_ref[0, :1, : step * lanes] < forwarders
            total = jnp.where(hands_on, held_refs[part][:, columns].astype(jnp.float32), total)
        out_refs[part][:, columns] = total.astype(out_refs[part].dtype)


def layer(pieces, matrix, offset, parts, late=0, place=None, forwarders=0, kept=()):
    pairs, width, lanes = matrix.shape
    batch, kind = pieces[0].shape[0], pieces[0].dtype
    outs = parts if pairs % parts == 0 else 1
    extra, kept = ([place], list(kept)) if forwarders else ([], [])
    early, pieces = (pieces[:-late], pieces[-late:]) if late else ([], pieces)
    if outs < parts:
        early, pieces, kept = [[jnp.concatenate(some, axis=1)] if some else [] for some in (early, pieces, kept)]
    params = pltpu.CompilerParams(vmem_limit_bytes=LAYER_VMEM)

    def cost(depth):
        flops, moved = 2 * batch * depth * pairs * lanes, 2 * pairs * depth * lanes
        return pl.CostEstimate(flops=flops, bytes_accessed=moved, transcendentals=0)

    depth = sum(piece.shape[1] for piece in early)
    start = offset
    if early:
        start = pl.pallas_call(
            early_kernel,
            in_specs=[WHOLE] * (len(early) + 2),
            out_specs=WHOLE,
            out_shape=jax.ShapeDtypeStruct((batch, pairs * lanes), jnp.float32),
            cost_estimate=cost(depth),
            compiler_params=params,
            name="layer_early",
        )(*early, matrix, offset)
    result = pl.pallas_call(
        functools.partial(layer_kernel, len(pieces), outs, depth, forwarders),
        in_specs=[WHOLE] * (len(pieces) + 2 + len(extra) + len(kept)),
        out_specs=[WHOLE] * outs,
        out_shape=[jax.ShapeDtypeStruct((batch, pairs * lanes // outs), kind)] * outs,
        cost_estimate=cost(width - depth),
        compiler_params=params,
        name="layer",
    )(*pieces, matrix, start, *extra, *kept)
    return list(result) if outs == parts else jnp.split(result[0], parts, axis=1)


def finish_kernel(place_ref, *refs):
    out_ref = refs[-1]
    deep, group, tile, batch = out_ref.shape
    part_refs, exchanged_refs = refs[:group], refs[group:-1]
    odd = place_ref[0, :1, :batch] % 2 == 1
    near = place_ref[1, :1, :batch]
    values = [part.T for part in [ref[...] for ref in part_refs]]
    for x in range(1, group):
        values[x] = jnp.where(odd, exchanged_refs[x - 1][...].T, values[x])
    for e in range(group):
        value = values[e]
        for digit in range(1, group):
            value = jnp.where(near == digit, values[e ^ digit], value)
        out_ref[:, e] = value.reshape(deep, tile, batch)


def finished(parts, exchanged, place, shape):
    return pl.pallas_call(
        finish_kernel,
        in_specs=[WHOLE] * (1 + len(parts) + len(exchanged)),
        out_specs=WHOLE,
        out_shape=jax.ShapeDtypeStruct(shape, parts[0].dtype),
        compiler_params=pltpu.CompilerParams(vmem_limit_bytes=LAYER_VMEM),
        name="finish",
    )(place, *parts, *exchanged)


def body(inputs, weights, biases, tile_index):
    micro_count, local, tile, batch = inputs.shape
    fan = tile_index.shape[2]
    segments, devices = lax.axis_size("segment"), lax.axis_size("blk")
    assert micro_count == segments and segments % 2 == 0
    group = min(local, devices // 4)
    deep = local // group
    part_width = deep * tile
    segment, position = lax.axis_index("segment"), lax.axis_index("blk")
    core, near, far = position & 1, (position >> 1) & (group - 1), position // (2 * group) & 1

    member = jnp.arange(fan, dtype=jnp.int32)
    member_digit, member_slot = member // local, member % local
    in_part = ((member_slot % group) ^ near) * deep + member_slot // group
    even_columns = (member_digit ^ core) * local + jnp.where(segment == 0, member_slot, in_part)
    part, across = (member_slot % group) ^ near, member_digit ^ far
    odd_piece = jnp.where(across == 0, jnp.where(part == 0, 0, 1 + part), jnp.where(part == 0, 1, group + part))
    odd_columns = odd_piece * deep + member_slot // group
    columns = jnp.stack([even_columns, odd_columns])
    spot = jnp.arange(local, dtype=jnp.int32)
    slots_of = spot % deep * group + ((spot // deep) ^ near)
    copies = max(1, deep // 2)
    order = sorted(range(local // 2), key=lambda pair: (2 * pair % deep, pair))
    place = jnp.broadcast_to(jnp.stack([segment, near]).astype(jnp.int32)[:, None, None], (2, 8, max(batch, 4 * tile)))
    columns, slots_of, place, first = lax.optimization_barrier((columns, slots_of, place, segment == 0))
    matrices = [placed(index, weights, tile_index, columns, slots_of, order, copies) for index in range(2)]
    layers = list(zip(matrices, rows_of(biases, place, group)))

    def along(value, flip):
        return lax.ppermute(value, "blk", [(i, i ^ flip) for i in range(devices)])

    def exchange(parts):
        pieces = {0: parts[0]}
        for x in range(1, 2 * group):
            pieces[x] = along(parts[x % group], 2 * x)
        return [pieces[x] for x in (0, group, *range(1, group), *range(group + 1, 2 * group))]

    def passed(parts):
        return [
            lax.ppermute(
                part,
                ("segment", "blk"),
                [(s * devices + i, (s + 1) % segments * devices + (i ^ 2 * x)) for s in range(segments) for i in range(devices)],
            )
            for x, part in enumerate(parts)
        ]

    sequence = [*range(segments - 2, -1, -1), segments - 1]
    turns = micro_count + segments - 1
    fresh = inputs.reshape(micro_count, local * tile, batch)
    arriving = ()
    for turn in range(turns):
        if turn == 0:
            pieces = turned([fresh, along(fresh, 1)], sequence[turn])
        elif turn < micro_count:
            (new,) = turned([fresh], sequence[turn])
            new = [new[:, x * part_width : (x + 1) * part_width] for x in range(group)]
            pieces = [jnp.where(first, a, b) for a, b in zip(new, arriving)]
        else:
            pieces = arriving
        if turn:
            pieces = pieces + [along(part, 1) for part in pieces]
        parts = layer(pieces, *layers[0], group, 1 if turn else 0)
        pieces = exchange(parts)
        forwarders = max(0, turn - micro_count + 1)
        parts = layer(pieces, *layers[1], group, 1, place, forwarders, arriving)
        if turn < turns - 1:
            arriving = passed(parts)

    exchanged = [along(parts[x], 2 * x) for x in range(1, group)]
    return finished(parts, exchanged, place, (deep, group, tile, batch)).reshape(1, local, tile, batch)


def solution(mesh):
    in_specs = (
        P(None, "blk", None, None),
        P("segment", "blk", None, None),
        P("segment", "blk", None),
        P("segment", "blk", None),
    )
    out_specs = P("segment", "blk", None, None)
    return jax.shard_map(body, mesh=mesh, in_specs=in_specs, out_specs=out_specs, check_vma=False)
```
